256 devices in a mesh: tm: 8 (over x, core), port: 32 (over y, z).
Axes of the slice: x: 4, y: 4, z: 8, core: 2. Of those that a mesh axis runs over, the one named last changes fastest.
Arguments:
- counters: bfloat16 [8192, 256], P('tm'), may hold values from -6 to 6
- signatures: bfloat16 [256, 8192], P(None, 'port'), may hold values from -0.375 to 0.375
- eigen_vectors_at_pins: bfloat16 [8192, 256], P('port'), may hold values from -0.125 to 0.125
- taps: bfloat16 [256, 4096], P('port'), may hold values from -0.5 to 0.5
Outputs:
- voltage_sag: bfloat16 [8192, 8192], P('tm', 'port')
The draws below stay inside these ranges and needn't reach their ends.
All inputs are finite; a program needn't handle non-finite values.
Results may differ from the reference program's by a relative error of at most 0.007.
Values may be sent and summed in bfloat16 or wider, within the bound.
No kernel may reach another device: no remote copies, remote signals or barrier semaphores. Data moves between devices by JAX's collectives and lax.ppermute only.
A program may use at most 128 MiB of HBM per device.

```python
import jax
import jax.numpy as jnp
from jax import lax

ACTIVITY_TALLIES = 256
PORTS = 8192
MODES = 256
TAPS = 4096
WINDOW_CYCLES = 8192


def spiked(drawn, key, source, target, blocks, factor):
    def block_of(dim):
        return (jnp.arange(drawn.shape[dim]) // (drawn.shape[dim] // blocks)).reshape((-1,) + (1,) * (drawn.ndim - 1 - dim))

    first = jax.random.permutation(key, blocks)[block_of(target)]
    second = (block_of(target) + blocks // 2) % blocks
    return jnp.where((block_of(source) == first) | (block_of(source) == second), factor * drawn, drawn)


def levels(rng, dims, split, least, high):
    level = 1.0
    for position, blocks in split:
        heights = jax.random.uniform(jax.random.fold_in(jax.random.fold_in(rng, 6), position), (blocks,), jnp.float32, least / len(split), high / len(split))
        level = level * jnp.repeat(jnp.exp(heights), dims[position] // blocks).reshape((-1,) + (1,) * (len(dims) - 1 - position))
    return level


def centred(key, dims, width, bound, shards=(), held_as=jnp.bfloat16):
    result = jax.random.normal(key, dims, jnp.float32) * width
    if len(shards) > 0:
        result = levels(key, dims, shards, -0.22, 0.18) * result
    return jnp.clip(result, min=-bound, max=bound).astype(held_as)


def gaussian_with(rng, shape, width, most, split, heavy, held_as=jnp.bfloat16):
    result = width * jax.random.normal(rng, shape, jnp.float32)
    if split:
        result = result * levels(rng, shape, split, -0.22, 0.18)
    return jnp.clip(spiked(result, jax.random.fold_in(rng, 3), *heavy), -most, most).astype(held_as)


def setup_inputs(seed: int = 0) -> dict:
    streams_of = jax.random.split(jax.random.key(seed), 5)
    return {
        "counters": centred(streams_of[0], (WINDOW_CYCLES, ACTIVITY_TALLIES), 1.0, 6.0, ((0, 8),)),
        "signatures": centred(streams_of[1], (ACTIVITY_TALLIES, PORTS), ACTIVITY_TALLIES ** -0.5, 0.375, ((1, 32),)),
        "eigen_vectors_at_pins": gaussian_with(streams_of[2], (PORTS, MODES), PORTS ** -0.5, 0.125, ((0, 32),), (0, 1, 32, 2.75)),
        "taps": centred(streams_of[3], (MODES, TAPS), (TAPS * MODES // PORTS) ** -0.5, 0.5, ((0, 32),)),
    }


def reference(counters, signatures, eigen_vectors_at_pins, taps):
    merged = jnp.dot(signatures, eigen_vectors_at_pins, preferred_element_type=jnp.float32)
    projected = jnp.dot(counters.astype(jnp.float32), merged, precision=lax.Precision.HIGHEST)
    modal = lax.optimization_barrier(projected.astype(jnp.bfloat16)).astype(jnp.float32).T
    length = WINDOW_CYCLES + TAPS
    spectrum = jnp.fft.rfft(modal, n=length, axis=1) * jnp.fft.rfft(taps.astype(jnp.float32), n=length, axis=1)
    kernel_taps_per_mode = jnp.fft.irfft(spectrum, n=length, axis=1)[:, :WINDOW_CYCLES].astype(jnp.bfloat16)
    voltage_sag = jnp.dot(kernel_taps_per_mode.T, eigen_vectors_at_pins.T, preferred_element_type=jnp.float32)
    return voltage_sag.astype(jnp.bfloat16)
```

```python
import functools

import jax
import jax.numpy as jnp
from jax import lax
from jax.experimental import pallas as pl
from jax.experimental.pallas import tpu as pltpu
from jax.sharding import PartitionSpec as P

LANES = 128
SUB = 8
STEP = 32
PER_TILE = LANES // STEP


def flipping_matrix():
    row = lax.broadcasted_iota(jnp.int32, (LANES, LANES), 0)
    col = lax.broadcasted_iota(jnp.int32, (LANES, LANES), 1)
    return jnp.where(row + col == LANES - 1, 1.0, 0.0).astype(jnp.bfloat16)


def toeplitz_kernel(tiles, depth, taps_ref, out_ref):
    modes = taps_ref.shape[0]
    stacked = jnp.concatenate(
        [taps_ref[:, LANES * (tiles - 1 - j) : LANES * (tiles - j)].astype(jnp.float32) for j in range(tiles)], axis=0
    )
    flipped = jnp.dot(stacked.astype(jnp.bfloat16), flipping_matrix(), preferred_element_type=jnp.float32)
    lane = lax.broadcasted_iota(jnp.int32, (SUB, LANES), 1)
    sub = lax.broadcasted_iota(jnp.int32, (SUB, LANES), 0)
    groups = STEP // SUB
    zero = jnp.zeros((SUB, LANES), jnp.float32)
    for m in range(modes):
        before = [zero] * groups
        for j in range(depth // LANES):
            if j < tiles:
                line = jnp.broadcast_to(flipped[modes * j + m : modes * j + m + 1, :], (SUB, LANES))
                now = [pltpu.roll(line, SUB * g + 1, 1, stride=1, stride_axis=0) for g in range(groups)]
            else:
                now = [zero] * groups
            parts = [
                jnp.where(lane < sub + (SUB * g + 1), before[g], now[g]) if j <= tiles else zero for g in range(groups)
            ]
            out_ref[STEP * m : STEP * (m + 1), LANES * j : LANES * (j + 1)] = jnp.concatenate(parts, axis=0).astype(
                out_ref.dtype
            )
            before = now


def projection_kernel(parts_ref, own_ref, other_ref, out_ref):
    merged = jnp.sum(parts_ref[...], axis=0)
    high = merged.astype(jnp.bfloat16).astype(jnp.float32)
    rest = merged - high
    middle = rest.astype(jnp.bfloat16).astype(jnp.float32)
    low = rest - middle
    modes = merged.shape[0]
    weights = jnp.concatenate([high, middle, low, jnp.zeros_like(low)], axis=0).astype(jnp.bfloat16)
    contract = (((1,), (1,)), ((), ()))

    def modal(ref):
        terms = lax.dot_general(weights, ref[...], contract, preferred_element_type=jnp.float32)
        return terms[:modes] + (terms[modes : 2 * modes] + terms[2 * modes : 3 * modes])

    own, other = modal(own_ref), modal(other_ref)
    first = lax.rem(lax.axis_index("tm"), 2) == 0
    span = own.shape[1]
    out_ref[:, :span] = jnp.where(first, own, other).astype(out_ref.dtype)
    out_ref[:, span:] = jnp.where(first, other, own).astype(out_ref.dtype)


def convolution_kernel(tap_tiles, copies, back2_ref, back1_ref, pair_ref, toeplitz_ref, out_ref, hankel):
    place = lax.axis_index("tm")
    chip, second = place // 2, lax.rem(place, 2) == 1
    modes, pair = pair_ref.shape
    span = pair // 2
    out_tiles = span // LANES
    older = jnp.where(chip >= 2, back2_ref[...].astype(jnp.float32), 0.0)
    newer = jnp.where(chip >= 1, back1_ref[...].astype(jnp.float32), 0.0)
    every = jnp.concatenate([older, newer, pair_ref[...].astype(jnp.float32)], axis=1)
    window = span + tap_tiles * LANES
    window = jnp.where(second, every[:, span : span + window], every[:, :window])
    count = window.shape[1] // LANES
    tiles = [window[:, LANES * t : LANES * (t + 1)] for t in range(count)]
    lane = lax.broadcasted_iota(jnp.int32, (SUB, LANES), 1)
    zero = jnp.zeros((SUB, LANES), jnp.float32)
    rolled = [[tile] + [pltpu.roll(tile, LANES - STEP * j, 1) for j in range(1, PER_TILE)] for tile in tiles]
    rolled.append([zero] * PER_TILE)
    for t in range(count):
        rows = [tiles[t]] + [
            jnp.where(lane < LANES - STEP * j, rolled[t][j], rolled[t + 1][j]) for j in range(1, PER_TILE)
        ]
        hankel[t] = jnp.concatenate(rows, axis=0).astype(hankel.dtype)
    for t in range(count, hankel.shape[0]):
        hankel[t] = jnp.zeros(hankel.shape[1:], hankel.dtype)
    depth = toeplitz_ref.shape[1]
    rows = out_tiles * PER_TILE * modes
    contract = (((1,), (1,)), ((), ()))
    total = jnp.zeros((rows, STEP * modes), jnp.float32)
    for c in range(0, depth // LANES, 2):
        left = jnp.concatenate(
            [hankel[c + k : c + k + out_tiles].reshape(rows, LANES) for k in range(2)], axis=1
        )
        total = total + lax.dot_general(
            left, toeplitz_ref[:, LANES * c : LANES * (c + 2)], contract, preferred_element_type=jnp.float32
        )
    sub = lax.broadcasted_iota(jnp.int32, (SUB, LANES), 0)
    place_in_tile, column = sub % PER_TILE, lane // STEP
    for g in range(out_tiles):
        picked = []
        for j in range(PER_TILE):
            row = (g * PER_TILE + j) * modes
            block = total[row : row + modes]
            own = block[:, :LANES]
            for h in range(1, STEP * modes // LANES):
                own = jnp.where(sub // PER_TILE == h, block[:, LANES * h : LANES * (h + 1)], own)
            picked.append(own)
        tile = zero
        for d in range(PER_TILE):
            line = picked[d]
            for s in range(1, PER_TILE):
                line = jnp.where(place_in_tile == s, picked[(s + d) % PER_TILE], line)
            if d:
                line = pltpu.roll(line, STEP * d, 1)
            tile = jnp.where(column == (place_in_tile + d) % PER_TILE, line, tile)
        tile = tile.astype(out_ref.dtype)
        for k in range(copies):
            out_ref[k, :, LANES * g : LANES * (g + 1)] = tile


def on_chip(kernel, shape, dtype, scratch=(), flops=0, bytes_accessed=0):
    return pl.pallas_call(
        kernel,
        out_shape=jax.ShapeDtypeStruct(shape, dtype),
        scratch_shapes=scratch,
        compiler_params=pltpu.CompilerParams(vmem_limit_bytes=40 * 1024 * 1024),
        cost_estimate=pl.CostEstimate(flops=flops, bytes_accessed=bytes_accessed, transcendentals=0),
    )


def per_device(ports, steps, counters, signatures, eigen_vectors_at_pins, taps):
    modes, span = taps.shape
    cycles, tallies = counters.shape
    swap = [(i, i ^ 1) for i in range(steps)]
    other = lax.ppermute(counters, "tm", swap)
    partial = jnp.einsum("cp,pm->mc", signatures, eigen_vectors_at_pins, preferred_element_type=jnp.float32)
    parts = lax.all_to_all(partial.reshape(ports, modes, tallies), "port", 0, 0, tiled=True)
    tap_tiles = span // LANES
    depth = (tap_tiles + 2) * LANES
    toeplitz = on_chip(
        functools.partial(toeplitz_kernel, tap_tiles, depth),
        (STEP * modes, depth),
        jnp.bfloat16,
        flops=2 * 10**9,
        bytes_accessed=2 * STEP * modes * depth,
    )(taps)
    pair = on_chip(projection_kernel, (modes, 2 * cycles), jnp.bfloat16)(parts, counters, other)
    back1 = lax.ppermute(pair, "tm", [(i, (i + 2) % steps) for i in range(steps)])
    back2 = lax.ppermute(pair, "tm", [(i, (i + 4) % steps) for i in range(steps)])
    responses = on_chip(
        functools.partial(convolution_kernel, tap_tiles, ports),
        (ports, modes, cycles),
        jnp.bfloat16,
        scratch=[pltpu.VMEM((tap_tiles + 1 + cycles // LANES + 1, PER_TILE * modes, LANES), jnp.bfloat16)],
    )(back2, back1, pair, toeplitz)
    complete = lax.all_to_all(responses, "port", 0, 0, tiled=True).reshape(ports * modes, cycles)
    return jnp.einsum("vm,uv->mu", complete, eigen_vectors_at_pins, preferred_element_type=jnp.float32).astype(
        jnp.bfloat16
    )


def solution(mesh):
    in_specs = (P("tm", None), P(None, "port"), P("port", None), P("port", None))
    body = functools.partial(per_device, mesh.shape["port"], mesh.shape["tm"])
    return jax.shard_map(body, mesh=mesh, in_specs=in_specs, out_specs=P("tm", "port"), check_vma=False)
```

```python
import functools

import jax
import jax.numpy as jnp
from jax import lax
from jax.experimental import pallas as pl
from jax.experimental.pallas import tpu as pltpu
from jax.sharding import PartitionSpec as P

LANES = 128
SUB = 8
STEP = 32
PER_TILE = LANES // STEP


def flipping_matrix():
    row = lax.broadcasted_iota(jnp.int32, (LANES, LANES), 0)
    col = lax.broadcasted_iota(jnp.int32, (LANES, LANES), 1)
    return jnp.where(row + col == LANES - 1, 1.0, 0.0).astype(jnp.bfloat16)


def toeplitz_kernel(tiles, depth, taps_ref, out_ref):
    modes = taps_ref.shape[0]
    stacked = jnp.concatenate(
        [taps_ref[:, LANES * (tiles - 1 - j) : LANES * (tiles - j)].astype(jnp.float32) for j in range(tiles)], axis=0
    )
    flipped = jnp.dot(stacked.astype(jnp.bfloat16), flipping_matrix(), preferred_element_type=jnp.float32)
    lane = lax.broadcasted_iota(jnp.int32, (SUB, LANES), 1)
    sub = lax.broadcasted_iota(jnp.int32, (SUB, LANES), 0)
    groups = STEP // SUB
    zero = jnp.zeros((SUB, LANES), jnp.float32)
    for m in range(modes):
        before = [zero] * groups
        for j in range(depth // LANES):
            if j < tiles:
                line = jnp.broadcast_to(flipped[modes * j + m : modes * j + m + 1, :], (SUB, LANES))
                now = [pltpu.roll(line, SUB * g + 1, 1, stride=1, stride_axis=0) for g in range(groups)]
            else:
                now = [zero] * groups
            parts = [
                jnp.where(lane < sub + (SUB * g + 1), before[g], now[g]) if j <= tiles else zero for g in range(groups)
            ]
            out_ref[STEP * m : STEP * (m + 1), LANES * j : LANES * (j + 1)] = jnp.concatenate(parts, axis=0).astype(
                out_ref.dtype
            )
            before = now


def merging_kernel(signatures_hbm, modes_hbm, counters_hbm, partial_ref, counters_ref, signatures_ref, modes_ref, sems):
    copies = [
        pltpu.make_async_copy(signatures_hbm, signatures_ref, sems.at[0]),
        pltpu.make_async_copy(modes_hbm, modes_ref, sems.at[1]),
        pltpu.make_async_copy(counters_hbm, counters_ref, sems.at[2]),
    ]
    for copy in copies:
        copy.start()
    copies[0].wait()
    copies[1].wait()
    partial = lax.dot_general(
        modes_ref[...], signatures_ref[...], (((0,), (1,)), ((), ())), preferred_element_type=jnp.float32
    )
    partial_ref[...] = partial.reshape(partial_ref.shape).astype(partial_ref.dtype)
    copies[2].wait()


def projection_kernel(parts_ref, own_ref, other_ref, out_ref):
    merged = jnp.sum(parts_ref[...].astype(jnp.float32), axis=0)
    high = merged.astype(jnp.bfloat16).astype(jnp.float32)
    rest = merged - high
    middle = rest.astype(jnp.bfloat16).astype(jnp.float32)
    low = rest - middle
    modes = merged.shape[0]
    weights = jnp.concatenate([high, middle, low, jnp.zeros_like(low)], axis=0).astype(jnp.bfloat16)
    contract = (((1,), (1,)), ((), ()))

    def modal(ref):
        terms = lax.dot_general(weights, ref[...], contract, preferred_element_type=jnp.float32)
        return terms[:modes] + (terms[modes : 2 * modes] + terms[2 * modes : 3 * modes])

    own, other = modal(own_ref), modal(other_ref)
    first = lax.rem(lax.axis_index("tm"), 2) == 0
    span = own.shape[1]
    out_ref[:, :span] = jnp.where(first, own, other).astype(out_ref.dtype)
    out_ref[:, span:] = jnp.where(first, other, own).astype(out_ref.dtype)


def convolution_kernel(tap_tiles, copies, back2_ref, back1_ref, pair_ref, toeplitz_ref, out_ref, hankel):
    place = lax.axis_index("tm")
    chip, second = place // 2, lax.rem(place, 2) == 1
    modes, pair = pair_ref.shape
    span = pair // 2
    out_tiles = span // LANES
    older = jnp.where(chip >= 2, back2_ref[...].astype(jnp.float32), 0.0)
    newer = jnp.where(chip >= 1, back1_ref[...].astype(jnp.float32), 0.0)
    every = jnp.concatenate([older, newer, pair_ref[...].astype(jnp.float32)], axis=1)
    window = span + tap_tiles * LANES
    window = jnp.where(second, every[:, span : span + window], every[:, :window])
    count = window.shape[1] // LANES
    tiles = [window[:, LANES * t : LANES * (t + 1)] for t in range(count)]
    lane = lax.broadcasted_iota(jnp.int32, (SUB, LANES), 1)
    zero = jnp.zeros((SUB, LANES), jnp.float32)
    rolled = [[tile] + [pltpu.roll(tile, LANES - STEP * j, 1) for j in range(1, PER_TILE)] for tile in tiles]
    rolled.append([zero] * PER_TILE)
    for t in range(count):
        rows = [tiles[t]] + [
            jnp.where(lane < LANES - STEP * j, rolled[t][j], rolled[t + 1][j]) for j in range(1, PER_TILE)
        ]
        hankel[t] = jnp.concatenate(rows, axis=0).astype(hankel.dtype)
    for t in range(count, hankel.shape[0]):
        hankel[t] = jnp.zeros(hankel.shape[1:], hankel.dtype)
    depth = toeplitz_ref.shape[1]
    rows = out_tiles * PER_TILE * modes
    contract = (((1,), (1,)), ((), ()))
    total = jnp.zeros((rows, STEP * modes), jnp.float32)
    for c in range(0, depth // LANES, 2):
        left = jnp.concatenate(
            [hankel[c + k : c + k + out_tiles].reshape(rows, LANES) for k in range(2)], axis=1
        )
        total = total + lax.dot_general(
            left, toeplitz_ref[:, LANES * c : LANES * (c + 2)], contract, preferred_element_type=jnp.float32
        )
    sub = lax.broadcasted_iota(jnp.int32, (SUB, LANES), 0)
    place_in_tile, column = sub % PER_TILE, lane // STEP
    for g in range(out_tiles):
        picked = []
        for j in range(PER_TILE):
            row = (g * PER_TILE + j) * modes
            block = total[row : row + modes]
            own = block[:, :LANES]
            for h in range(1, STEP * modes // LANES):
                own = jnp.where(sub // PER_TILE == h, block[:, LANES * h : LANES * (h + 1)], own)
            picked.append(own)
        tile = zero
        for d in range(PER_TILE):
            line = picked[d]
            for s in range(1, PER_TILE):
                line = jnp.where(place_in_tile == s, picked[(s + d) % PER_TILE], line)
            if d:
                line = pltpu.roll(line, STEP * d, 1)
            tile = jnp.where(column == (place_in_tile + d) % PER_TILE, line, tile)
        tile = tile.astype(out_ref.dtype)
        for k in range(copies):
            out_ref[k, :, LANES * g : LANES * (g + 1)] = tile


def on_chip(kernel, shape, dtype, scratch=(), flops=0, bytes_accessed=0):
    return pl.pallas_call(
        kernel,
        out_shape=jax.ShapeDtypeStruct(shape, dtype),
        scratch_shapes=scratch,
        compiler_params=pltpu.CompilerParams(vmem_limit_bytes=40 * 1024 * 1024),
        cost_estimate=pl.CostEstimate(flops=flops, bytes_accessed=bytes_accessed, transcendentals=0),
    )


def per_device(ports, steps, counters, signatures, eigen_vectors_at_pins, taps):
    modes, span = taps.shape
    cycles, tallies = counters.shape
    swap = [(i, i ^ 1) for i in range(steps)]
    other = lax.ppermute(counters, "tm", swap)
    in_hbm = pl.BlockSpec(memory_space=pltpu.HBM)
    in_vmem = pl.BlockSpec(memory_space=pltpu.VMEM)
    partial, held = pl.pallas_call(
        merging_kernel,
        out_shape=(
            jax.ShapeDtypeStruct((ports, modes, tallies), jnp.bfloat16),
            jax.ShapeDtypeStruct(counters.shape, counters.dtype),
        ),
        in_specs=[in_hbm] * 3,
        out_specs=(in_vmem, in_vmem),
        scratch_shapes=[
            pltpu.VMEM(signatures.shape, signatures.dtype),
            pltpu.VMEM(eigen_vectors_at_pins.shape, eigen_vectors_at_pins.dtype),
            pltpu.SemaphoreType.DMA((3,)),
        ],
        compiler_params=pltpu.CompilerParams(vmem_limit_bytes=16 * 1024 * 1024),
    )(*[pltpu.with_memory_space_constraint(x, pltpu.HBM) for x in (signatures, eigen_vectors_at_pins, counters)])
    parts = lax.all_to_all(partial, "port", 0, 0, tiled=True)
    tap_tiles = span // LANES
    depth = (tap_tiles + 2) * LANES
    toeplitz = on_chip(
        functools.partial(toeplitz_kernel, tap_tiles, depth),
        (STEP * modes, depth),
        jnp.bfloat16,
        flops=2 * 10**9,
        bytes_accessed=2 * STEP * modes * depth,
    )(taps)
    pair = on_chip(projection_kernel, (modes, 2 * cycles), jnp.bfloat16)(parts, held, other)
    back2 = lax.ppermute(pair, "tm", [(i, (i + 4) % steps) for i in range(steps)])
    back1 = lax.ppermute(pair, "tm", [(i, (i + 2) % steps) for i in range(steps)])
    responses = on_chip(
        functools.partial(convolution_kernel, tap_tiles, ports),
        (ports, modes, cycles),
        jnp.bfloat16,
        scratch=[pltpu.VMEM((tap_tiles + 1 + cycles // LANES + 1, PER_TILE * modes, LANES), jnp.bfloat16)],
    )(back2, back1, pair, toeplitz)
    complete = lax.all_to_all(responses, "port", 0, 0, tiled=True).reshape(ports * modes, cycles)
    return jnp.einsum("vm,uv->mu", complete, eigen_vectors_at_pins, preferred_element_type=jnp.float32).astype(
        jnp.bfloat16
    )


def solution(mesh):
    in_specs = (P("tm", None), P(None, "port"), P("port", None), P("port", None))
    body = functools.partial(per_device, mesh.shape["port"], mesh.shape["tm"])
    return jax.shard_map(body, mesh=mesh, in_specs=in_specs, out_specs=P("tm", "port"), check_vma=False)
```

```python
import functools

import jax
import jax.numpy as jnp
from jax import lax
from jax.experimental import pallas as pl
from jax.experimental.pallas import tpu as pltpu
from jax.sharding import PartitionSpec as P

LANES = 128
SUB = 8
STEP = 32
PER_TILE = LANES // STEP


def flipping_matrix():
    row = lax.broadcasted_iota(jnp.int32, (LANES, LANES), 0)
    col = lax.broadcasted_iota(jnp.int32, (LANES, LANES), 1)
    return jnp.where(row + col == LANES - 1, 1.0, 0.0).astype(jnp.bfloat16)


def fill_toeplitz(tiles, depth, taps_ref, out_ref):
    modes = taps_ref.shape[0]
    stacked = jnp.concatenate(
        [taps_ref[:, LANES * (tiles - 1 - j) : LANES * (tiles - j)].astype(jnp.float32) for j in range(tiles)], axis=0
    )
    flipped = jnp.dot(stacked.astype(jnp.bfloat16), flipping_matrix(), preferred_element_type=jnp.float32)
    lane = lax.broadcasted_iota(jnp.int32, (SUB, LANES), 1)
    sub = lax.broadcasted_iota(jnp.int32, (SUB, LANES), 0)
    groups = STEP // SUB
    zero = jnp.zeros((SUB, LANES), jnp.float32)
    for m in range(modes):
        before = [zero] * groups
        for j in range(depth // LANES):
            if j < tiles:
                line = jnp.broadcast_to(flipped[modes * j + m : modes * j + m + 1, :], (SUB, LANES))
                now = [pltpu.roll(line, SUB * g + 1, 1, stride=1, stride_axis=0) for g in range(groups)]
            else:
                now = [zero] * groups
            parts = [
                jnp.where(lane < sub + (SUB * g + 1), before[g], now[g]) if j <= tiles else zero for g in range(groups)
            ]
            out_ref[STEP * m : STEP * (m + 1), LANES * j : LANES * (j + 1)] = jnp.concatenate(parts, axis=0).astype(
                out_ref.dtype
            )
            before = now


def merging_kernel(signatures_hbm, modes_hbm, counters_hbm, partial_ref, counters_ref, signatures_ref, modes_ref, sems):
    copies = [
        pltpu.make_async_copy(signatures_hbm, signatures_ref, sems.at[0]),
        pltpu.make_async_copy(modes_hbm, modes_ref, sems.at[1]),
        pltpu.make_async_copy(counters_hbm, counters_ref, sems.at[2]),
    ]
    for copy in copies:
        copy.start()
    copies[0].wait()
    copies[1].wait()
    partial = lax.dot_general(
        modes_ref[...], signatures_ref[...], (((0,), (1,)), ((), ())), preferred_element_type=jnp.float32
    )
    partial_ref[...] = partial.reshape(partial_ref.shape).astype(partial_ref.dtype)
    copies[2].wait()


def projection_kernel(parts_ref, own_ref, other_ref, out_ref):
    merged = jnp.sum(parts_ref[...].astype(jnp.float32), axis=0)
    high = merged.astype(jnp.bfloat16).astype(jnp.float32)
    rest = merged - high
    middle = rest.astype(jnp.bfloat16).astype(jnp.float32)
    low = rest - middle
    modes = merged.shape[0]
    weights = jnp.concatenate([high, middle, low, jnp.zeros_like(low)], axis=0).astype(jnp.bfloat16)
    contract = (((1,), (1,)), ((), ()))

    def modal(ref):
        terms = lax.dot_general(weights, ref[...], contract, preferred_element_type=jnp.float32)
        return terms[:modes] + (terms[modes : 2 * modes] + terms[2 * modes : 3 * modes])

    own, other = modal(own_ref), modal(other_ref)
    first = lax.rem(lax.axis_index("tm"), 2) == 0
    span = own.shape[1]
    out_ref[:, :span] = jnp.where(first, own, other).astype(out_ref.dtype)
    out_ref[:, span:] = jnp.where(first, other, own).astype(out_ref.dtype)


def hankel_rows(tiles, following):
    lane = lax.broadcasted_iota(jnp.int32, (SUB, LANES), 1)
    moved = [[pltpu.roll(tile, LANES - STEP * j, 1) for j in range(1, PER_TILE)] for tile in [*tiles, following]]
    for t, tile in enumerate(tiles):
        rows = [tile] + [
            jnp.where(lane < LANES - STEP * j, moved[t][j - 1], moved[t + 1][j - 1]) for j in range(1, PER_TILE)
        ]
        yield jnp.concatenate(rows, axis=0)


def banded_product(total, hankel, first, toeplitz_ref, steps, out_tiles):
    rows = total.shape[0]
    for c in steps:
        left = jnp.concatenate(
            [hankel[c + k - first : c + k - first + out_tiles].reshape(rows, LANES) for k in range(2)], axis=1
        )
        total = total + lax.dot_general(
            left,
            toeplitz_ref[:, LANES * c : LANES * (c + 2)],
            (((1,), (1,)), ((), ())),
            preferred_element_type=jnp.float32,
        )
    return total


def near_kernel(out_tiles, back1_ref, pair_ref, taps_ref, total_ref, hankel_ref, toeplitz_ref):
    fill_toeplitz(taps_ref.shape[1] // LANES, toeplitz_ref.shape[1], taps_ref, toeplitz_ref)
    place = lax.axis_index("tm")
    chip, second = place // 2, lax.rem(place, 2) == 1
    span = out_tiles * LANES
    newer = jnp.where(chip >= 1, back1_ref[...].astype(jnp.float32), 0.0)
    every = jnp.concatenate([newer, pair_ref[...].astype(jnp.float32)], axis=1)
    known = every.shape[1] - span
    window = jnp.where(second, every[:, span:], every[:, :known])
    count = known // LANES
    tiles = [window[:, LANES * t : LANES * (t + 1)] for t in range(count)]
    for t, rows in enumerate(hankel_rows(tiles, jnp.zeros((SUB, LANES), jnp.float32))):
        hankel_ref[t] = rows.astype(hankel_ref.dtype)
    for t in range(count, hankel_ref.shape[0]):
        hankel_ref[t] = jnp.zeros(hankel_ref.shape[1:], hankel_ref.dtype)
    first = 2 * out_tiles
    steps = range(first, toeplitz_ref.shape[1] // LANES, 2)
    total_ref[...] = banded_product(jnp.zeros(total_ref.shape, jnp.float32), hankel_ref, first, toeplitz_ref, steps, out_tiles)


def far_kernel(out_tiles, copies, back2_ref, back1_ref, near_ref, near_hankel_ref, toeplitz_ref, out_ref, hankel):
    place = lax.axis_index("tm")
    chip, second = place // 2, lax.rem(place, 2) == 1
    modes = out_ref.shape[1]
    span = out_tiles * LANES
    older = jnp.where(chip >= 2, back2_ref[...].astype(jnp.float32), 0.0)
    newer = jnp.where(chip >= 1, back1_ref[:, : span + LANES].astype(jnp.float32), 0.0)
    every = jnp.concatenate([older, newer], axis=1)
    first = 2 * out_tiles
    width = first * LANES + LANES
    window = jnp.where(second, every[:, span : span + width], every[:, :width])
    tiles = [window[:, LANES * t : LANES * (t + 1)] for t in range(first)]
    for t, rows in enumerate(hankel_rows(tiles, window[:, first * LANES :])):
        hankel[t] = rows.astype(hankel.dtype)
    hankel[first:] = near_hankel_ref[: hankel.shape[0] - first]
    total = banded_product(near_ref[...], hankel, 0, toeplitz_ref, range(0, first, 2), out_tiles)
    lane = lax.broadcasted_iota(jnp.int32, (SUB, LANES), 1)
    sub = lax.broadcasted_iota(jnp.int32, (SUB, LANES), 0)
    place_in_tile, column = sub % PER_TILE, lane // STEP
    for g in range(out_tiles):
        picked = []
        for j in range(PER_TILE):
            row = (g * PER_TILE + j) * modes
            block = total[row : row + modes]
            own = block[:, :LANES]
            for h in range(1, STEP * modes // LANES):
                own = jnp.where(sub // PER_TILE == h, block[:, LANES * h : LANES * (h + 1)], own)
            picked.append(own)
        tile = jnp.zeros((SUB, LANES), jnp.float32)
        for d in range(PER_TILE):
            line = picked[d]
            for s in range(1, PER_TILE):
                line = jnp.where(place_in_tile == s, picked[(s + d) % PER_TILE], line)
            if d:
                line = pltpu.roll(line, STEP * d, 1)
            tile = jnp.where(column == (place_in_tile + d) % PER_TILE, line, tile)
        tile = tile.astype(out_ref.dtype)
        for k in range(copies):
            out_ref[k, :, LANES * g : LANES * (g + 1)] = tile


def sag_kernel(responses_ref, modes_ref, out_hbm, blocks_ref, sems):
    blocks, span = blocks_ref.shape[:2]
    modes = modes_ref[...]
    copies = []
    for k in range(blocks):
        part = responses_ref[:, :, span * k : span * (k + 1)].reshape(modes.shape[1], span)
        product = lax.dot_general(part, modes, (((0,), (1,)), ((), ())), preferred_element_type=jnp.float32)
        blocks_ref[k] = product.astype(blocks_ref.dtype)
        copies.append(pltpu.make_async_copy(blocks_ref.at[k], out_hbm.at[pl.ds(span * k, span)], sems.at[k]))
        copies[-1].start()
    for copy in copies:
        copy.wait()


def on_chip(kernel, shape, dtype, scratch=(), flops=0, bytes_accessed=0):
    return pl.pallas_call(
        kernel,
        out_shape=jax.ShapeDtypeStruct(shape, dtype),
        scratch_shapes=scratch,
        compiler_params=pltpu.CompilerParams(vmem_limit_bytes=40 * 1024 * 1024),
        cost_estimate=pl.CostEstimate(flops=flops, bytes_accessed=bytes_accessed, transcendentals=0),
    )


def per_device(ports, steps, counters, signatures, eigen_vectors_at_pins, taps):
    modes, span = taps.shape
    cycles, tallies = counters.shape
    swap = [(i, i ^ 1) for i in range(steps)]
    other = lax.ppermute(counters, "tm", swap)
    in_hbm = pl.BlockSpec(memory_space=pltpu.HBM)
    in_vmem = pl.BlockSpec(memory_space=pltpu.VMEM)
    partial, held = pl.pallas_call(
        merging_kernel,
        out_shape=(
            jax.ShapeDtypeStruct((ports, modes, tallies), jnp.bfloat16),
            jax.ShapeDtypeStruct(counters.shape, counters.dtype),
        ),
        in_specs=[in_hbm] * 3,
        out_specs=(in_vmem, in_vmem),
        scratch_shapes=[
            pltpu.VMEM(signatures.shape, signatures.dtype),
            pltpu.VMEM(eigen_vectors_at_pins.shape, eigen_vectors_at_pins.dtype),
            pltpu.SemaphoreType.DMA((3,)),
        ],
        compiler_params=pltpu.CompilerParams(vmem_limit_bytes=16 * 1024 * 1024),
    )(*[pltpu.with_memory_space_constraint(x, pltpu.HBM) for x in (signatures, eigen_vectors_at_pins, counters)])
    parts = lax.all_to_all(partial, "port", 0, 0, tiled=True)
    tap_tiles = span // LANES
    depth = (tap_tiles + 2) * LANES
    pair = on_chip(projection_kernel, (modes, 2 * cycles), jnp.bfloat16)(parts, held, other)
    back2 = lax.ppermute(pair, "tm", [(i, (i + 4) % steps) for i in range(steps)])
    back1 = lax.ppermute(pair, "tm", [(i, (i + 2) % steps) for i in range(steps)])
    out_tiles = cycles // LANES
    rows = STEP * modes
    near, near_hankel, toeplitz = pl.pallas_call(
        functools.partial(near_kernel, out_tiles),
        out_shape=(
            jax.ShapeDtypeStruct((out_tiles * PER_TILE * modes, rows), jnp.float32),
            jax.ShapeDtypeStruct((tap_tiles + 2 - out_tiles, PER_TILE * modes, LANES), jnp.bfloat16),
            jax.ShapeDtypeStruct((rows, depth), jnp.bfloat16),
        ),
        compiler_params=pltpu.CompilerParams(vmem_limit_bytes=40 * 1024 * 1024),
        cost_estimate=pl.CostEstimate(flops=2 * 10**9, bytes_accessed=4 * rows * depth, transcendentals=0),
    )(back1, pair, taps)
    responses = on_chip(
        functools.partial(far_kernel, out_tiles, ports),
        (ports, modes, cycles),
        jnp.bfloat16,
        scratch=[pltpu.VMEM((3 * out_tiles, PER_TILE * modes, LANES), jnp.bfloat16)],
    )(back2, back1, near, near_hankel, toeplitz)
    complete = lax.all_to_all(responses, "port", 0, 0, tiled=True)
    local_ports = eigen_vectors_at_pins.shape[0]
    blocks = 4
    return pl.pallas_call(
        sag_kernel,
        out_shape=jax.ShapeDtypeStruct((cycles, local_ports), jnp.bfloat16),
        in_specs=[in_vmem] * 2,
        out_specs=pl.BlockSpec(memory_space=pltpu.HBM),
        scratch_shapes=[
            pltpu.VMEM((blocks, cycles // blocks, local_ports), jnp.bfloat16),
            pltpu.SemaphoreType.DMA((blocks,)),
        ],
        compiler_params=pltpu.CompilerParams(vmem_limit_bytes=16 * 1024 * 1024),
    )(complete, eigen_vectors_at_pins)


def solution(mesh):
    in_specs = (P("tm", None), P(None, "port"), P("port", None), P("port", None))
    body = functools.partial(per_device, mesh.shape["port"], mesh.shape["tm"])
    return jax.shard_map(body, mesh=mesh, in_specs=in_specs, out_specs=P("tm", "port"), check_vma=False)
```

```python
import functools

import jax
import jax.numpy as jnp
from jax import lax
from jax.experimental import pallas as pl
from jax.experimental.pallas import tpu as pltpu
from jax.sharding import PartitionSpec as P

LANES = 128
SUB = 8
STEP = 32
PER_TILE = LANES // STEP


def flipping_matrix():
    row = lax.broadcasted_iota(jnp.int32, (LANES, LANES), 0)
    col = lax.broadcasted_iota(jnp.int32, (LANES, LANES), 1)
    return jnp.where(row + col == LANES - 1, 1.0, 0.0).astype(jnp.bfloat16)


def fill_toeplitz(tiles, depth, taps_ref, out_ref):
    modes = taps_ref.shape[0]
    stacked = jnp.concatenate(
        [taps_ref[:, LANES * (tiles - 1 - j) : LANES * (tiles - j)].astype(jnp.float32) for j in range(tiles)], axis=0
    )
    flipped = jnp.dot(stacked.astype(jnp.bfloat16), flipping_matrix(), preferred_element_type=jnp.float32)
    lane = lax.broadcasted_iota(jnp.int32, (SUB, LANES), 1)
    sub = lax.broadcasted_iota(jnp.int32, (SUB, LANES), 0)
    groups = STEP // SUB
    zero = jnp.zeros((SUB, LANES), jnp.float32)
    for m in range(modes):
        before = [zero] * groups
        for j in range(depth // LANES):
            if j < tiles:
                line = jnp.broadcast_to(flipped[modes * j + m : modes * j + m + 1, :], (SUB, LANES))
                now = [pltpu.roll(line, SUB * g + 1, 1, stride=1, stride_axis=0) for g in range(groups)]
            else:
                now = [zero] * groups
            parts = [
                jnp.where(lane < sub + (SUB * g + 1), before[g], now[g]) if j <= tiles else zero for g in range(groups)
            ]
            out_ref[STEP * m : STEP * (m + 1), LANES * j : LANES * (j + 1)] = jnp.concatenate(parts, axis=0).astype(
                out_ref.dtype
            )
            before = now


def is_second():
    return lax.rem(lax.axis_index("tm"), 2) == 1


def merging_kernel(
    signatures_hbm,
    modes_hbm,
    counters_hbm,
    taps_hbm,
    partial_ref,
    counters_ref,
    toeplitz_ref,
    signatures_ref,
    modes_ref,
    taps_ref,
    sems,
):
    copies = [
        pltpu.make_async_copy(signatures_hbm, signatures_ref, sems.at[0]),
        pltpu.make_async_copy(modes_hbm, modes_ref, sems.at[1]),
        pltpu.make_async_copy(taps_hbm, taps_ref, sems.at[2]),
        pltpu.make_async_copy(counters_hbm, counters_ref, sems.at[3]),
    ]
    for copy in copies:
        copy.start()
    copies[2].wait()

    @pl.when(jnp.logical_not(is_second()))
    def _():
        fill_toeplitz(taps_ref.shape[1] // LANES, toeplitz_ref.shape[1], taps_ref, toeplitz_ref)

    copies[0].wait()
    copies[1].wait()
    partial = lax.dot_general(
        modes_ref[...], signatures_ref[...], (((0,), (1,)), ((), ())), preferred_element_type=jnp.float32
    )
    partial_ref[...] = partial.reshape(partial_ref.shape).astype(partial_ref.dtype)

    copies[3].wait()


def projection_kernel(parts_ref, own_ref, other_ref, out_ref):
    merged = jnp.sum(parts_ref[...].astype(jnp.float32), axis=0)
    high = merged.astype(jnp.bfloat16).astype(jnp.float32)
    rest = merged - high
    middle = rest.astype(jnp.bfloat16).astype(jnp.float32)
    low = rest - middle
    modes = merged.shape[0]
    weights = jnp.concatenate([high, middle, low, jnp.zeros_like(low)], axis=0).astype(jnp.bfloat16)
    contract = (((1,), (1,)), ((), ()))

    def modal(ref):
        terms = lax.dot_general(weights, ref[...], contract, preferred_element_type=jnp.float32)
        return terms[:modes] + (terms[modes : 2 * modes] + terms[2 * modes : 3 * modes])

    own, other = modal(own_ref), modal(other_ref)
    first = jnp.logical_not(is_second())
    span = own.shape[1]
    out_ref[:, :span] = jnp.where(first, own, other).astype(out_ref.dtype)
    out_ref[:, span:] = jnp.where(first, other, own).astype(out_ref.dtype)


def hankel_rows(tiles, following):
    lane = lax.broadcasted_iota(jnp.int32, (SUB, LANES), 1)
    moved = [[pltpu.roll(tile, LANES - STEP * j, 1) for j in range(1, PER_TILE)] for tile in [*tiles, following]]
    for t, tile in enumerate(tiles):
        rows = [tile] + [
            jnp.where(lane < LANES - STEP * j, moved[t][j - 1], moved[t + 1][j - 1]) for j in range(1, PER_TILE)
        ]
        yield jnp.concatenate(rows, axis=0)


def banded_product(total, hankel, first, toeplitz_ref, steps, out_tiles):
    rows = total.shape[0]
    for c in steps:
        left = jnp.concatenate(
            [hankel[c + k - first : c + k - first + out_tiles].reshape(rows, LANES) for k in range(2)], axis=1
        )
        total = total + lax.dot_general(
            left,
            toeplitz_ref[:, LANES * c : LANES * (c + 2)],
            (((1,), (1,)), ((), ())),
            preferred_element_type=jnp.float32,
        )
    return total


def near_kernel(out_tiles, back1_ref, pair_ref, taps_ref, formed_ref, total_ref, hankel_ref, toeplitz_ref):
    del formed_ref

    @pl.when(is_second())
    def _():
        fill_toeplitz(taps_ref.shape[1] // LANES, toeplitz_ref.shape[1], taps_ref, toeplitz_ref)

    place = lax.axis_index("tm")
    chip, second = place // 2, lax.rem(place, 2) == 1
    span = out_tiles * LANES
    newer = jnp.where(chip >= 1, back1_ref[...].astype(jnp.float32), 0.0)
    every = jnp.concatenate([newer, pair_ref[...].astype(jnp.float32)], axis=1)
    known = every.shape[1] - span
    window = jnp.where(second, every[:, span:], every[:, :known])
    count = known // LANES
    tiles = [window[:, LANES * t : LANES * (t + 1)] for t in range(count)]
    for t, rows in enumerate(hankel_rows(tiles, jnp.zeros((SUB, LANES), jnp.float32))):
        hankel_ref[t] = rows.astype(hankel_ref.dtype)
    for t in range(count, hankel_ref.shape[0]):
        hankel_ref[t] = jnp.zeros(hankel_ref.shape[1:], hankel_ref.dtype)
    first = 2 * out_tiles
    steps = range(first, toeplitz_ref.shape[1] // LANES, 2)
    total_ref[...] = banded_product(jnp.zeros(total_ref.shape, jnp.float32), hankel_ref, first, toeplitz_ref, steps, out_tiles)


def far_kernel(out_tiles, copies, back2_ref, back1_ref, near_ref, near_hankel_ref, toeplitz_ref, out_ref, hankel):
    place = lax.axis_index("tm")
    chip, second = place // 2, lax.rem(place, 2) == 1
    modes = out_ref.shape[1]
    span = out_tiles * LANES
    older = jnp.where(chip >= 2, back2_ref[...].astype(jnp.float32), 0.0)
    newer = jnp.where(chip >= 1, back1_ref[:, : span + LANES].astype(jnp.float32), 0.0)
    every = jnp.concatenate([older, newer], axis=1)
    first = 2 * out_tiles
    width = first * LANES + LANES
    window = jnp.where(second, every[:, span : span + width], every[:, :width])
    tiles = [window[:, LANES * t : LANES * (t + 1)] for t in range(first)]
    for t, rows in enumerate(hankel_rows(tiles, window[:, first * LANES :])):
        hankel[t] = rows.astype(hankel.dtype)
    hankel[first:] = near_hankel_ref[: hankel.shape[0] - first]
    total = banded_product(near_ref[...], hankel, 0, toeplitz_ref, range(0, first, 2), out_tiles)
    lane = lax.broadcasted_iota(jnp.int32, (SUB, LANES), 1)
    sub = lax.broadcasted_iota(jnp.int32, (SUB, LANES), 0)
    place_in_tile, column = sub % PER_TILE, lane // STEP
    for g in range(out_tiles):
        picked = []
        for j in range(PER_TILE):
            row = (g * PER_TILE + j) * modes
            block = total[row : row + modes]
            own = block[:, :LANES]
            for h in range(1, STEP * modes // LANES):
                own = jnp.where(sub // PER_TILE == h, block[:, LANES * h : LANES * (h + 1)], own)
            picked.append(own)
        tile = jnp.zeros((SUB, LANES), jnp.float32)
        for d in range(PER_TILE):
            line = picked[d]
            for s in range(1, PER_TILE):
                line = jnp.where(place_in_tile == s, picked[(s + d) % PER_TILE], line)
            if d:
                line = pltpu.roll(line, STEP * d, 1)
            tile = jnp.where(column == (place_in_tile + d) % PER_TILE, line, tile)
        tile = tile.astype(out_ref.dtype)
        for k in range(copies):
            out_ref[k, :, LANES * g : LANES * (g + 1)] = tile


def sag_kernel(responses_ref, modes_ref, out_hbm, blocks_ref, sems):
    blocks, span = blocks_ref.shape[:2]
    modes = modes_ref[...]
    copies = []
    for k in range(blocks):
        part = responses_ref[:, :, span * k : span * (k + 1)].reshape(modes.shape[1], span)
        product = lax.dot_general(part, modes, (((0,), (1,)), ((), ())), preferred_element_type=jnp.float32)
        blocks_ref[k] = product.astype(blocks_ref.dtype)
        copies.append(pltpu.make_async_copy(blocks_ref.at[k], out_hbm.at[pl.ds(span * k, span)], sems.at[k]))
        copies[-1].start()
    for copy in copies:
        copy.wait()


def on_chip(kernel, shape, dtype, scratch=(), flops=0, bytes_accessed=0):
    return pl.pallas_call(
        kernel,
        out_shape=jax.ShapeDtypeStruct(shape, dtype),
        scratch_shapes=scratch,
        compiler_params=pltpu.CompilerParams(vmem_limit_bytes=40 * 1024 * 1024),
        cost_estimate=pl.CostEstimate(flops=flops, bytes_accessed=bytes_accessed, transcendentals=0),
    )


def per_device(ports, steps, counters, signatures, eigen_vectors_at_pins, taps):
    modes, span = taps.shape
    cycles, tallies = counters.shape
    swap = [(i, i ^ 1) for i in range(steps)]
    other = lax.ppermute(counters, "tm", swap)
    in_hbm = pl.BlockSpec(memory_space=pltpu.HBM)
    in_vmem = pl.BlockSpec(memory_space=pltpu.VMEM)
    depth = span + 2 * LANES
    partial, held, formed = pl.pallas_call(
        merging_kernel,
        out_shape=(
            jax.ShapeDtypeStruct((ports, modes, tallies), jnp.bfloat16),
            jax.ShapeDtypeStruct(counters.shape, counters.dtype),
            jax.ShapeDtypeStruct((STEP * modes, depth), jnp.bfloat16),
        ),
        in_specs=[in_hbm] * 4,
        out_specs=(in_vmem,) * 3,
        scratch_shapes=[
            pltpu.VMEM(signatures.shape, signatures.dtype),
            pltpu.VMEM(eigen_vectors_at_pins.shape, eigen_vectors_at_pins.dtype),
            pltpu.VMEM(taps.shape, taps.dtype),
            pltpu.SemaphoreType.DMA((4,)),
        ],
        compiler_params=pltpu.CompilerParams(vmem_limit_bytes=16 * 1024 * 1024),
    )(*[pltpu.with_memory_space_constraint(x, pltpu.HBM) for x in (signatures, eigen_vectors_at_pins, counters, taps)])
    parts = lax.all_to_all(partial, "port", 0, 0, tiled=True)
    tap_tiles = span // LANES
    pair = on_chip(projection_kernel, (modes, 2 * cycles), jnp.bfloat16)(parts, held, other)
    back2 = lax.ppermute(pair, "tm", [(i, (i + 4) % steps) for i in range(steps)])
    back1 = lax.ppermute(pair, "tm", [(i, (i + 2) % steps) for i in range(steps)])
    out_tiles = cycles // LANES
    rows = STEP * modes
    near, near_hankel, toeplitz = pl.pallas_call(
        functools.partial(near_kernel, out_tiles),
        out_shape=(
            jax.ShapeDtypeStruct((out_tiles * PER_TILE * modes, rows), jnp.float32),
            jax.ShapeDtypeStruct((tap_tiles + 2 - out_tiles, PER_TILE * modes, LANES), jnp.bfloat16),
            jax.ShapeDtypeStruct((rows, depth), jnp.bfloat16),
        ),
        input_output_aliases={3: 2},
        compiler_params=pltpu.CompilerParams(vmem_limit_bytes=40 * 1024 * 1024),
        cost_estimate=pl.CostEstimate(flops=2 * 10**9, bytes_accessed=4 * rows * depth, transcendentals=0),
    )(back1, pair, taps, formed)
    responses = on_chip(
        functools.partial(far_kernel, out_tiles, ports),
        (ports, modes, cycles),
        jnp.bfloat16,
        scratch=[pltpu.VMEM((3 * out_tiles, PER_TILE * modes, LANES), jnp.bfloat16)],
    )(back2, back1, near, near_hankel, toeplitz)
    complete = lax.all_to_all(responses, "port", 0, 0, tiled=True)
    local_ports = eigen_vectors_at_pins.shape[0]
    blocks = 4
    return pl.pallas_call(
        sag_kernel,
        out_shape=jax.ShapeDtypeStruct((cycles, local_ports), jnp.bfloat16),
        in_specs=[in_vmem] * 2,
        out_specs=pl.BlockSpec(memory_space=pltpu.HBM),
        scratch_shapes=[
            pltpu.VMEM((blocks, cycles // blocks, local_ports), jnp.bfloat16),
            pltpu.SemaphoreType.DMA((blocks,)),
        ],
        compiler_params=pltpu.CompilerParams(vmem_limit_bytes=16 * 1024 * 1024),
    )(complete, eigen_vectors_at_pins)


def solution(mesh):
    in_specs = (P("tm", None), P(None, "port"), P("port", None), P("port", None))
    body = functools.partial(per_device, mesh.shape["port"], mesh.shape["tm"])
    return jax.shard_map(body, mesh=mesh, in_specs=in_specs, out_specs=P("tm", "port"), check_vma=False)
```

```python
import functools

import jax
import jax.numpy as jnp
from jax import lax
from jax.experimental import pallas as pl
from jax.experimental.pallas import tpu as pltpu
from jax.sharding import PartitionSpec as P

LANES = 128
SUB = 8
STEP = 32
PER_TILE = LANES // STEP


def flipping_matrix():
    row = lax.broadcasted_iota(jnp.int32, (LANES, LANES), 0)
    col = lax.broadcasted_iota(jnp.int32, (LANES, LANES), 1)
    return jnp.where(row + col == LANES - 1, 1.0, 0.0).astype(jnp.bfloat16)


def fill_toeplitz(tiles, depth, taps_ref, out_ref):
    modes = taps_ref.shape[0]
    stacked = jnp.concatenate(
        [taps_ref[:, LANES * (tiles - 1 - j) : LANES * (tiles - j)].astype(jnp.float32) for j in range(tiles)], axis=0
    )
    flipped = jnp.dot(stacked.astype(jnp.bfloat16), flipping_matrix(), preferred_element_type=jnp.float32)
    lane = lax.broadcasted_iota(jnp.int32, (SUB, LANES), 1)
    sub = lax.broadcasted_iota(jnp.int32, (SUB, LANES), 0)
    groups = STEP // SUB
    zero = jnp.zeros((SUB, LANES), jnp.float32)
    for m in range(modes):
        before = [zero] * groups
        for j in range(depth // LANES):
            if j < tiles:
                line = jnp.broadcast_to(flipped[modes * j + m : modes * j + m + 1, :], (SUB, LANES))
                now = [pltpu.roll(line, SUB * g + 1, 1, stride=1, stride_axis=0) for g in range(groups)]
            else:
                now = [zero] * groups
            parts = [
                jnp.where(lane < sub + (SUB * g + 1), before[g], now[g]) if j <= tiles else zero for g in range(groups)
            ]
            out_ref[STEP * m : STEP * (m + 1), LANES * j : LANES * (j + 1)] = jnp.concatenate(parts, axis=0).astype(
                out_ref.dtype
            )
            before = now


def is_second():
    return lax.rem(lax.axis_index("tm"), 2) == 1


def merging_kernel(
    signatures_hbm,
    modes_hbm,
    counters_hbm,
    taps_hbm,
    partial_ref,
    counters_ref,
    toeplitz_ref,
    signatures_ref,
    modes_ref,
    taps_ref,
    sems,
):
    copies = [
        pltpu.make_async_copy(signatures_hbm, signatures_ref, sems.at[0]),
        pltpu.make_async_copy(modes_hbm, modes_ref, sems.at[1]),
        pltpu.make_async_copy(taps_hbm, taps_ref, sems.at[2]),
        pltpu.make_async_copy(counters_hbm, counters_ref, sems.at[3]),
    ]
    for copy in copies:
        copy.start()
    copies[2].wait()

    @pl.when(jnp.logical_not(is_second()))
    def _():
        fill_toeplitz(taps_ref.shape[1] // LANES, toeplitz_ref.shape[1], taps_ref, toeplitz_ref)

    copies[0].wait()
    copies[1].wait()
    partial = lax.dot_general(
        modes_ref[...], signatures_ref[...], (((0,), (1,)), ((), ())), preferred_element_type=jnp.float32
    )
    partial_ref[...] = partial.reshape(partial_ref.shape).astype(partial_ref.dtype)

    copies[3].wait()


def projection_kernel(parts_ref, own_ref, other_ref, out_ref):
    merged = jnp.sum(parts_ref[...].astype(jnp.float32), axis=0)
    high = merged.astype(jnp.bfloat16).astype(jnp.float32)
    rest = merged - high
    middle = rest.astype(jnp.bfloat16).astype(jnp.float32)
    low = rest - middle
    modes = merged.shape[0]
    weights = jnp.concatenate([high, middle, low, jnp.zeros_like(low)], axis=0).astype(jnp.bfloat16)
    contract = (((1,), (1,)), ((), ()))

    def modal(ref):
        terms = lax.dot_general(weights, ref[...], contract, preferred_element_type=jnp.float32)
        return terms[:modes] + (terms[modes : 2 * modes] + terms[2 * modes : 3 * modes])

    own, other = modal(own_ref), modal(other_ref)
    first = jnp.logical_not(is_second())
    span = own.shape[1]
    out_ref[:, :span] = jnp.where(first, own, other).astype(out_ref.dtype)
    out_ref[:, span:] = jnp.where(first, other, own).astype(out_ref.dtype)


def hankel_rows(tiles, following):
    lane = lax.broadcasted_iota(jnp.int32, (SUB, LANES), 1)
    moved = [[pltpu.roll(tile, LANES - STEP * j, 1) for j in range(1, PER_TILE)] for tile in [*tiles, following]]
    for t, tile in enumerate(tiles):
        rows = [tile] + [
            jnp.where(lane < LANES - STEP * j, moved[t][j - 1], moved[t + 1][j - 1]) for j in range(1, PER_TILE)
        ]
        yield jnp.concatenate(rows, axis=0)


def banded_product(total, hankel, first, toeplitz_ref, steps, out_tiles):
    rows = total.shape[0]
    for c in steps:
        left = jnp.concatenate(
            [hankel[c + k - first : c + k - first + out_tiles].reshape(rows, LANES) for k in range(2)], axis=1
        )
        total = total + lax.dot_general(
            left,
            toeplitz_ref[:, LANES * c : LANES * (c + 2)],
            (((1,), (1,)), ((), ())),
            preferred_element_type=jnp.float32,
        )
    return total


def near_kernel(out_tiles, back1_ref, pair_ref, taps_ref, formed_ref, total_ref, hankel_ref, toeplitz_ref):
    del formed_ref

    @pl.when(is_second())
    def _():
        fill_toeplitz(taps_ref.shape[1] // LANES, toeplitz_ref.shape[1], taps_ref, toeplitz_ref)

    chip = lax.axis_index("tm") // 2
    newer = jnp.where(chip >= 1, back1_ref[...].astype(jnp.float32), 0.0)
    every = jnp.concatenate([newer, pair_ref[...].astype(jnp.float32)], axis=1)

    def give(first):
        count = toeplitz_ref.shape[1] // LANES + out_tiles - 2 - first
        tiles = [every[:, LANES * t : LANES * (t + 1)] for t in range(count)]
        for t, rows in enumerate(hankel_rows(tiles, jnp.zeros((SUB, LANES), jnp.float32))):
            hankel_ref[first - out_tiles + t] = rows.astype(hankel_ref.dtype)
        for t in range(first - out_tiles + count, hankel_ref.shape[0]):
            hankel_ref[t] = jnp.zeros(hankel_ref.shape[1:], hankel_ref.dtype)
        steps = range(first, toeplitz_ref.shape[1] // LANES, 2)
        nothing = jnp.zeros(total_ref.shape, jnp.float32)
        total_ref[...] = banded_product(nothing, hankel_ref, out_tiles, toeplitz_ref, steps, out_tiles)

    pl.when(is_second())(lambda: give(out_tiles))
    pl.when(jnp.logical_not(is_second()))(lambda: give(2 * out_tiles))


def far_kernel(
    out_tiles, copies, back2_ref, back1_ref, near_ref, near_hankel_ref, toeplitz_ref, out_ref, hankel, total_ref
):
    chip = lax.axis_index("tm") // 2
    modes = out_ref.shape[1]
    older = jnp.where(chip >= 2, back2_ref[...].astype(jnp.float32), 0.0)
    following = jnp.where(chip >= 1, back1_ref[:, :LANES].astype(jnp.float32), 0.0)

    def add(first):
        start = 2 * out_tiles - first
        tiles = [older[:, LANES * t : LANES * (t + 1)] for t in range(start, 2 * out_tiles)]
        for t, rows in enumerate(hankel_rows(tiles, following)):
            hankel[t] = rows.astype(hankel.dtype)
        hankel[first : first + out_tiles] = near_hankel_ref[first - out_tiles : first]
        total_ref[...] = banded_product(near_ref[...], hankel, 0, toeplitz_ref, range(0, first, 2), out_tiles)

    pl.when(is_second())(lambda: add(out_tiles))
    pl.when(jnp.logical_not(is_second()))(lambda: add(2 * out_tiles))
    total = total_ref[...]
    lane = lax.broadcasted_iota(jnp.int32, (SUB, LANES), 1)
    sub = lax.broadcasted_iota(jnp.int32, (SUB, LANES), 0)
    place_in_tile, column = sub % PER_TILE, lane // STEP
    for g in range(out_tiles):
        picked = []
        for j in range(PER_TILE):
            row = (g * PER_TILE + j) * modes
            block = total[row : row + modes]
            own = block[:, :LANES]
            for h in range(1, STEP * modes // LANES):
                own = jnp.where(sub // PER_TILE == h, block[:, LANES * h : LANES * (h + 1)], own)
            picked.append(own)
        tile = jnp.zeros((SUB, LANES), jnp.float32)
        for d in range(PER_TILE):
            line = picked[d]
            for s in range(1, PER_TILE):
                line = jnp.where(place_in_tile == s, picked[(s + d) % PER_TILE], line)
            if d:
                line = pltpu.roll(line, STEP * d, 1)
            tile = jnp.where(column == (place_in_tile + d) % PER_TILE, line, tile)
        tile = tile.astype(out_ref.dtype)
        for k in range(copies):
            out_ref[k, :, LANES * g : LANES * (g + 1)] = tile


def sag_kernel(responses_ref, modes_ref, out_hbm, blocks_ref, sems):
    blocks, span = blocks_ref.shape[:2]
    modes = modes_ref[...]
    copies = []
    for k in range(blocks):
        part = responses_ref[:, :, span * k : span * (k + 1)].reshape(modes.shape[1], span)
        product = lax.dot_general(part, modes, (((0,), (1,)), ((), ())), preferred_element_type=jnp.float32)
        blocks_ref[k] = product.astype(blocks_ref.dtype)
        copies.append(pltpu.make_async_copy(blocks_ref.at[k], out_hbm.at[pl.ds(span * k, span)], sems.at[k]))
        copies[-1].start()
    for copy in copies:
        copy.wait()


def on_chip(kernel, shape, dtype, scratch=(), flops=0, bytes_accessed=0):
    return pl.pallas_call(
        kernel,
        out_shape=jax.ShapeDtypeStruct(shape, dtype),
        scratch_shapes=scratch,
        compiler_params=pltpu.CompilerParams(vmem_limit_bytes=40 * 1024 * 1024),
        cost_estimate=pl.CostEstimate(flops=flops, bytes_accessed=bytes_accessed, transcendentals=0),
    )


def per_device(ports, steps, counters, signatures, eigen_vectors_at_pins, taps):
    modes, span = taps.shape
    cycles, tallies = counters.shape
    swap = [(i, i ^ 1) for i in range(steps)]
    other = lax.ppermute(counters, "tm", swap)
    in_hbm = pl.BlockSpec(memory_space=pltpu.HBM)
    in_vmem = pl.BlockSpec(memory_space=pltpu.VMEM)
    depth = span + 2 * LANES
    partial, held, formed = pl.pallas_call(
        merging_kernel,
        out_shape=(
            jax.ShapeDtypeStruct((ports, modes, tallies), jnp.bfloat16),
            jax.ShapeDtypeStruct(counters.shape, counters.dtype),
            jax.ShapeDtypeStruct((STEP * modes, depth), jnp.bfloat16),
        ),
        in_specs=[in_hbm] * 4,
        out_specs=(in_vmem,) * 3,
        scratch_shapes=[
            pltpu.VMEM(signatures.shape, signatures.dtype),
            pltpu.VMEM(eigen_vectors_at_pins.shape, eigen_vectors_at_pins.dtype),
            pltpu.VMEM(taps.shape, taps.dtype),
            pltpu.SemaphoreType.DMA((4,)),
        ],
        compiler_params=pltpu.CompilerParams(vmem_limit_bytes=16 * 1024 * 1024),
    )(*[pltpu.with_memory_space_constraint(x, pltpu.HBM) for x in (signatures, eigen_vectors_at_pins, counters, taps)])
    parts = lax.all_to_all(partial, "port", 0, 0, tiled=True)
    tap_tiles = span // LANES
    pair = on_chip(projection_kernel, (modes, 2 * cycles), jnp.bfloat16)(parts, held, other)
    back2 = lax.ppermute(pair, "tm", [(i, (i + 4) % steps) for i in range(steps)])
    back1 = lax.ppermute(pair, "tm", [(i, (i + 2) % steps) for i in range(steps)])
    out_tiles = cycles // LANES
    rows = STEP * modes
    near, near_hankel, toeplitz = pl.pallas_call(
        functools.partial(near_kernel, out_tiles),
        out_shape=(
            jax.ShapeDtypeStruct((out_tiles * PER_TILE * modes, rows), jnp.float32),
            jax.ShapeDtypeStruct((tap_tiles + 2, PER_TILE * modes, LANES), jnp.bfloat16),
            jax.ShapeDtypeStruct((rows, depth), jnp.bfloat16),
        ),
        input_output_aliases={3: 2},
        compiler_params=pltpu.CompilerParams(vmem_limit_bytes=40 * 1024 * 1024),
        cost_estimate=pl.CostEstimate(flops=2 * 10**9, bytes_accessed=4 * rows * depth, transcendentals=0),
    )(back1, pair, taps, formed)
    responses = on_chip(
        functools.partial(far_kernel, out_tiles, ports),
        (ports, modes, cycles),
        jnp.bfloat16,
        scratch=[
            pltpu.VMEM((3 * out_tiles, PER_TILE * modes, LANES), jnp.bfloat16),
            pltpu.VMEM((out_tiles * PER_TILE * modes, rows), jnp.float32),
        ],
    )(back2, back1, near, near_hankel, toeplitz)
    complete = lax.all_to_all(responses, "port", 0, 0, tiled=True)
    local_ports = eigen_vectors_at_pins.shape[0]
    blocks = 4
    return pl.pallas_call(
        sag_kernel,
        out_shape=jax.ShapeDtypeStruct((cycles, local_ports), jnp.bfloat16),
        in_specs=[in_vmem] * 2,
        out_specs=pl.BlockSpec(memory_space=pltpu.HBM),
        scratch_shapes=[
            pltpu.VMEM((blocks, cycles // blocks, local_ports), jnp.bfloat16),
            pltpu.SemaphoreType.DMA((blocks,)),
        ],
        compiler_params=pltpu.CompilerParams(vmem_limit_bytes=16 * 1024 * 1024),
    )(complete, eigen_vectors_at_pins)


def solution(mesh):
    in_specs = (P("tm", None), P(None, "port"), P("port", None), P("port", None))
    body = functools.partial(per_device, mesh.shape["port"], mesh.shape["tm"])
    return jax.shard_map(body, mesh=mesh, in_specs=in_specs, out_specs=P("tm", "port"), check_vma=False)
```

```python
import functools

import jax
import jax.numpy as jnp
from jax import lax
from jax.experimental import pallas as pl
from jax.experimental.pallas import tpu as pltpu
from jax.sharding import PartitionSpec as P

LANES = 128
SUB = 8
STEP = 32
PER_TILE = LANES // STEP


def flipping_matrix():
    row = lax.broadcasted_iota(jnp.int32, (LANES, LANES), 0)
    col = lax.broadcasted_iota(jnp.int32, (LANES, LANES), 1)
    return jnp.where(row + col == LANES - 1, 1.0, 0.0).astype(jnp.bfloat16)


def fill_toeplitz(tiles, depth, taps_ref, out_ref):
    modes = taps_ref.shape[0]
    stacked = jnp.concatenate(
        [taps_ref[:, LANES * (tiles - 1 - j) : LANES * (tiles - j)].astype(jnp.float32) for j in range(tiles)], axis=0
    )
    flipped = jnp.dot(stacked.astype(jnp.bfloat16), flipping_matrix(), preferred_element_type=jnp.float32)
    lane = lax.broadcasted_iota(jnp.int32, (SUB, LANES), 1)
    sub = lax.broadcasted_iota(jnp.int32, (SUB, LANES), 0)
    groups = STEP // SUB
    zero = jnp.zeros((SUB, LANES), jnp.float32)
    for m in range(modes):
        before = [zero] * groups
        for j in range(depth // LANES):
            if j < tiles:
                line = jnp.broadcast_to(flipped[modes * j + m : modes * j + m + 1, :], (SUB, LANES))
                now = [pltpu.roll(line, SUB * g + 1, 1, stride=1, stride_axis=0) for g in range(groups)]
            else:
                now = [zero] * groups
            parts = [
                jnp.where(lane < sub + (SUB * g + 1), before[g], now[g]) if j <= tiles else zero for g in range(groups)
            ]
            out_ref[STEP * m : STEP * (m + 1), LANES * j : LANES * (j + 1)] = jnp.concatenate(parts, axis=0).astype(
                out_ref.dtype
            )
            before = now


def is_second():
    return lax.rem(lax.axis_index("tm"), 2) == 1


def merging_kernel(
    signatures_hbm,
    modes_hbm,
    counters_hbm,
    taps_hbm,
    partial_ref,
    counters_ref,
    toeplitz_ref,
    signatures_ref,
    modes_ref,
    taps_ref,
    sems,
):
    copies = [
        pltpu.make_async_copy(signatures_hbm, signatures_ref, sems.at[0]),
        pltpu.make_async_copy(modes_hbm, modes_ref, sems.at[1]),
        pltpu.make_async_copy(taps_hbm, taps_ref, sems.at[2]),
        pltpu.make_async_copy(counters_hbm, counters_ref, sems.at[3]),
    ]
    for k in (2, 0, 1, 3):
        copies[k].start()
    copies[2].wait()

    @pl.when(jnp.logical_not(is_second()))
    def _():
        fill_toeplitz(taps_ref.shape[1] // LANES, toeplitz_ref.shape[1], taps_ref, toeplitz_ref)

    copies[0].wait()
    copies[1].wait()
    partial = lax.dot_general(
        modes_ref[...], signatures_ref[...], (((0,), (1,)), ((), ())), preferred_element_type=jnp.float32
    )
    partial_ref[...] = partial.reshape(partial_ref.shape).astype(partial_ref.dtype)

    copies[3].wait()


def projection_kernel(parts_ref, own_ref, other_ref, out_ref):
    merged = jnp.sum(parts_ref[...].astype(jnp.float32), axis=0)
    high = merged.astype(jnp.bfloat16).astype(jnp.float32)
    rest = merged - high
    middle = rest.astype(jnp.bfloat16).astype(jnp.float32)
    low = rest - middle
    modes = merged.shape[0]
    weights = jnp.concatenate([high, middle, low, jnp.zeros_like(low)], axis=0).astype(jnp.bfloat16)
    contract = (((1,), (1,)), ((), ()))

    def modal(ref):
        terms = lax.dot_general(weights, ref[...], contract, preferred_element_type=jnp.float32)
        return terms[:modes] + (terms[modes : 2 * modes] + terms[2 * modes : 3 * modes])

    own, other = modal(own_ref), modal(other_ref)
    first = jnp.logical_not(is_second())
    span = own.shape[1]
    out_ref[:, :span] = jnp.where(first, own, other).astype(out_ref.dtype)
    out_ref[:, span:] = jnp.where(first, other, own).astype(out_ref.dtype)


def hankel_rows(tiles, following):
    lane = lax.broadcasted_iota(jnp.int32, (SUB, LANES), 1)
    moved = [[pltpu.roll(tile, LANES - STEP * j, 1) for j in range(1, PER_TILE)] for tile in [*tiles, following]]
    for t, tile in enumerate(tiles):
        rows = [tile] + [
            jnp.where(lane < LANES - STEP * j, moved[t][j - 1], moved[t + 1][j - 1]) for j in range(1, PER_TILE)
        ]
        yield jnp.concatenate(rows, axis=0)


def banded_product(total, hankel, first, toeplitz_ref, steps, out_tiles):
    rows = total.shape[0]
    for c in steps:
        left = jnp.concatenate(
            [hankel[c + k - first : c + k - first + out_tiles].reshape(rows, LANES) for k in range(2)], axis=1
        )
        total = total + lax.dot_general(
            left,
            toeplitz_ref[:, LANES * c : LANES * (c + 2)],
            (((1,), (1,)), ((), ())),
            preferred_element_type=jnp.float32,
        )
    return total


def near_kernel(out_tiles, back1_ref, pair_ref, taps_ref, formed_ref, total_ref, hankel_ref, toeplitz_ref):
    del formed_ref

    @pl.when(is_second())
    def _():
        fill_toeplitz(taps_ref.shape[1] // LANES, toeplitz_ref.shape[1], taps_ref, toeplitz_ref)

    chip = lax.axis_index("tm") // 2
    newer = jnp.where(chip >= 1, back1_ref[...].astype(jnp.float32), 0.0)
    every = jnp.concatenate([newer, pair_ref[...].astype(jnp.float32)], axis=1)

    def give(first):
        count = toeplitz_ref.shape[1] // LANES + out_tiles - 2 - first
        tiles = [every[:, LANES * t : LANES * (t + 1)] for t in range(count)]
        for t, rows in enumerate(hankel_rows(tiles, jnp.zeros((SUB, LANES), jnp.float32))):
            hankel_ref[first - out_tiles + t] = rows.astype(hankel_ref.dtype)
        for t in range(first - out_tiles + count, hankel_ref.shape[0]):
            hankel_ref[t] = jnp.zeros(hankel_ref.shape[1:], hankel_ref.dtype)
        steps = range(first, toeplitz_ref.shape[1] // LANES, 2)
        nothing = jnp.zeros(total_ref.shape, jnp.float32)
        total_ref[...] = banded_product(nothing, hankel_ref, out_tiles, toeplitz_ref, steps, out_tiles)

    pl.when(is_second())(lambda: give(out_tiles))
    pl.when(jnp.logical_not(is_second()))(lambda: give(2 * out_tiles))


def far_kernel(
    out_tiles, copies, back2_ref, back1_ref, near_ref, near_hankel_ref, toeplitz_ref, out_ref, hankel, total_ref
):
    chip = lax.axis_index("tm") // 2
    modes = out_ref.shape[1]
    older = jnp.where(chip >= 2, back2_ref[...].astype(jnp.float32), 0.0)
    following = jnp.where(chip >= 1, back1_ref[:, :LANES].astype(jnp.float32), 0.0)

    def add(first):
        start = 2 * out_tiles - first
        tiles = [older[:, LANES * t : LANES * (t + 1)] for t in range(start, 2 * out_tiles)]
        for t, rows in enumerate(hankel_rows(tiles, following)):
            hankel[t] = rows.astype(hankel.dtype)
        hankel[first : first + out_tiles] = near_hankel_ref[first - out_tiles : first]
        total_ref[...] = banded_product(near_ref[...], hankel, 0, toeplitz_ref, range(0, first, 2), out_tiles)

    pl.when(is_second())(lambda: add(out_tiles))
    pl.when(jnp.logical_not(is_second()))(lambda: add(2 * out_tiles))
    total = total_ref[...]
    lane = lax.broadcasted_iota(jnp.int32, (SUB, LANES), 1)
    sub = lax.broadcasted_iota(jnp.int32, (SUB, LANES), 0)
    place_in_tile, column = sub % PER_TILE, lane // STEP
    for g in range(out_tiles):
        picked = []
        for j in range(PER_TILE):
            row = (g * PER_TILE + j) * modes
            block = total[row : row + modes]
            own = block[:, :LANES]
            for h in range(1, STEP * modes // LANES):
                own = jnp.where(sub // PER_TILE == h, block[:, LANES * h : LANES * (h + 1)], own)
            picked.append(own)
        tile = jnp.zeros((SUB, LANES), jnp.float32)
        for d in range(PER_TILE):
            line = picked[d]
            for s in range(1, PER_TILE):
                line = jnp.where(place_in_tile == s, picked[(s + d) % PER_TILE], line)
            if d:
                line = pltpu.roll(line, STEP * d, 1)
            tile = jnp.where(column == (place_in_tile + d) % PER_TILE, line, tile)
        tile = tile.astype(out_ref.dtype)
        for k in range(copies):
            out_ref[k, :, LANES * g : LANES * (g + 1)] = tile


def sag_kernel(responses_ref, modes_ref, out_hbm, blocks_ref, sems):
    blocks, span = blocks_ref.shape[:2]
    modes = modes_ref[...]
    copies = []
    for k in range(blocks):
        part = responses_ref[:, :, span * k : span * (k + 1)].reshape(modes.shape[1], span)
        product = lax.dot_general(part, modes, (((0,), (1,)), ((), ())), preferred_element_type=jnp.float32)
        blocks_ref[k] = product.astype(blocks_ref.dtype)
        copies.append(pltpu.make_async_copy(blocks_ref.at[k], out_hbm.at[pl.ds(span * k, span)], sems.at[k]))
        copies[-1].start()
    for copy in copies:
        copy.wait()


def on_chip(kernel, shape, dtype, scratch=(), flops=0, bytes_accessed=0):
    return pl.pallas_call(
        kernel,
        out_shape=jax.ShapeDtypeStruct(shape, dtype),
        scratch_shapes=scratch,
        compiler_params=pltpu.CompilerParams(vmem_limit_bytes=40 * 1024 * 1024),
        cost_estimate=pl.CostEstimate(flops=flops, bytes_accessed=bytes_accessed, transcendentals=0),
    )


def per_device(ports, steps, counters, signatures, eigen_vectors_at_pins, taps):
    modes, span = taps.shape
    cycles, tallies = counters.shape
    swap = [(i, i ^ 1) for i in range(steps)]
    other = lax.ppermute(counters, "tm", swap)
    in_hbm = pl.BlockSpec(memory_space=pltpu.HBM)
    in_vmem = pl.BlockSpec(memory_space=pltpu.VMEM)
    depth = span + 2 * LANES
    partial, held, formed = pl.pallas_call(
        merging_kernel,
        out_shape=(
            jax.ShapeDtypeStruct((ports, modes, tallies), jnp.bfloat16),
            jax.ShapeDtypeStruct(counters.shape, counters.dtype),
            jax.ShapeDtypeStruct((STEP * modes, depth), jnp.bfloat16),
        ),
        in_specs=[in_hbm] * 4,
        out_specs=(in_vmem,) * 3,
        scratch_shapes=[
            pltpu.VMEM(signatures.shape, signatures.dtype),
            pltpu.VMEM(eigen_vectors_at_pins.shape, eigen_vectors_at_pins.dtype),
            pltpu.VMEM(taps.shape, taps.dtype),
            pltpu.SemaphoreType.DMA((4,)),
        ],
        compiler_params=pltpu.CompilerParams(vmem_limit_bytes=16 * 1024 * 1024),
    )(*[pltpu.with_memory_space_constraint(x, pltpu.HBM) for x in (signatures, eigen_vectors_at_pins, counters, taps)])
    parts = lax.all_to_all(partial, "port", 0, 0, tiled=True)
    tap_tiles = span // LANES
    pair = on_chip(projection_kernel, (modes, 2 * cycles), jnp.bfloat16)(parts, held, other)
    back2 = lax.ppermute(pair, "tm", [(i, (i + 4) % steps) for i in range(steps)])
    back1 = lax.ppermute(pair, "tm", [(i, (i + 2) % steps) for i in range(steps)])
    out_tiles = cycles // LANES
    rows = STEP * modes
    near, near_hankel, toeplitz = pl.pallas_call(
        functools.partial(near_kernel, out_tiles),
        out_shape=(
            jax.ShapeDtypeStruct((out_tiles * PER_TILE * modes, rows), jnp.float32),
            jax.ShapeDtypeStruct((tap_tiles + 2, PER_TILE * modes, LANES), jnp.bfloat16),
            jax.ShapeDtypeStruct((rows, depth), jnp.bfloat16),
        ),
        input_output_aliases={3: 2},
        compiler_params=pltpu.CompilerParams(vmem_limit_bytes=40 * 1024 * 1024),
        cost_estimate=pl.CostEstimate(flops=2 * 10**9, bytes_accessed=4 * rows * depth, transcendentals=0),
    )(back1, pair, taps, formed)
    responses = on_chip(
        functools.partial(far_kernel, out_tiles, ports),
        (ports, modes, cycles),
        jnp.bfloat16,
        scratch=[
            pltpu.VMEM((3 * out_tiles, PER_TILE * modes, LANES), jnp.bfloat16),
            pltpu.VMEM((out_tiles * PER_TILE * modes, rows), jnp.float32),
        ],
    )(back2, back1, near, near_hankel, toeplitz)
    complete = lax.all_to_all(responses, "port", 0, 0, tiled=True)
    local_ports = eigen_vectors_at_pins.shape[0]
    blocks = 4
    return pl.pallas_call(
        sag_kernel,
        out_shape=jax.ShapeDtypeStruct((cycles, local_ports), jnp.bfloat16),
        in_specs=[in_vmem] * 2,
        out_specs=pl.BlockSpec(memory_space=pltpu.HBM),
        scratch_shapes=[
            pltpu.VMEM((blocks, cycles // blocks, local_ports), jnp.bfloat16),
            pltpu.SemaphoreType.DMA((blocks,)),
        ],
        compiler_params=pltpu.CompilerParams(vmem_limit_bytes=16 * 1024 * 1024),
    )(complete, eigen_vectors_at_pins)


def solution(mesh):
    in_specs = (P("tm", None), P(None, "port"), P("port", None), P("port", None))
    body = functools.partial(per_device, mesh.shape["port"], mesh.shape["tm"])
    return jax.shard_map(body, mesh=mesh, in_specs=in_specs, out_specs=P("tm", "port"), check_vma=False)
```

```python
import functools

import jax
import jax.numpy as jnp
from jax import lax
from jax.experimental import pallas as pl
from jax.experimental.pallas import tpu as pltpu
from jax.sharding import PartitionSpec as P

LANES = 128
SUB = 8
STEP = 32
PER_TILE = LANES // STEP


def flipping_matrix():
    row = lax.broadcasted_iota(jnp.int32, (LANES, LANES), 0)
    col = lax.broadcasted_iota(jnp.int32, (LANES, LANES), 1)
    return jnp.where(row + col == LANES - 1, 1.0, 0.0).astype(jnp.bfloat16)


def fill_toeplitz(tiles, depth, taps_ref, out_ref):
    modes = taps_ref.shape[0]
    stacked = jnp.concatenate(
        [taps_ref[:, LANES * (tiles - 1 - j) : LANES * (tiles - j)].astype(jnp.float32) for j in range(tiles)], axis=0
    )
    flipped = jnp.dot(stacked.astype(jnp.bfloat16), flipping_matrix(), preferred_element_type=jnp.float32)
    lane = lax.broadcasted_iota(jnp.int32, (SUB, LANES), 1)
    sub = lax.broadcasted_iota(jnp.int32, (SUB, LANES), 0)
    groups = STEP // SUB
    zero = jnp.zeros((SUB, LANES), jnp.float32)
    for m in range(modes):
        before = [zero] * groups
        for j in range(depth // LANES):
            if j < tiles:
                line = jnp.broadcast_to(flipped[modes * j + m : modes * j + m + 1, :], (SUB, LANES))
                now = [pltpu.roll(line, SUB * g + 1, 1, stride=1, stride_axis=0) for g in range(groups)]
            else:
                now = [zero] * groups
            parts = [
                jnp.where(lane < sub + (SUB * g + 1), before[g], now[g]) if j <= tiles else zero for g in range(groups)
            ]
            out_ref[STEP * m : STEP * (m + 1), LANES * j : LANES * (j + 1)] = jnp.concatenate(parts, axis=0).astype(
                out_ref.dtype
            )
            before = now


def is_second():
    return lax.rem(lax.axis_index("tm"), 2) == 1


def merging_kernel(
    signatures_hbm,
    modes_hbm,
    counters_hbm,
    taps_hbm,
    partial_ref,
    counters_ref,
    toeplitz_ref,
    signatures_ref,
    modes_ref,
    taps_ref,
    sems,
):
    copies = [
        pltpu.make_async_copy(signatures_hbm, signatures_ref, sems.at[0]),
        pltpu.make_async_copy(modes_hbm, modes_ref, sems.at[1]),
        pltpu.make_async_copy(taps_hbm, taps_ref, sems.at[2]),
        pltpu.make_async_copy(counters_hbm, counters_ref, sems.at[3]),
    ]
    for copy in copies:
        copy.start()
    copies[0].wait()
    copies[1].wait()
    partial = lax.dot_general(
        modes_ref[...], signatures_ref[...], (((0,), (1,)), ((), ())), preferred_element_type=jnp.float32
    )
    partial_ref[...] = partial.reshape(partial_ref.shape).astype(partial_ref.dtype)

    copies[2].wait()

    @pl.when(jnp.logical_not(is_second()))
    def _():
        fill_toeplitz(taps_ref.shape[1] // LANES, toeplitz_ref.shape[1], taps_ref, toeplitz_ref)

    copies[3].wait()


def projection_kernel(parts_ref, own_ref, other_ref, out_ref):
    merged = jnp.sum(parts_ref[...].astype(jnp.float32), axis=0)
    high = merged.astype(jnp.bfloat16).astype(jnp.float32)
    rest = merged - high
    middle = rest.astype(jnp.bfloat16).astype(jnp.float32)
    low = rest - middle
    modes = merged.shape[0]
    weights = jnp.concatenate([high, middle, low, jnp.zeros_like(low)], axis=0).astype(jnp.bfloat16)
    contract = (((1,), (1,)), ((), ()))

    def modal(ref):
        terms = lax.dot_general(weights, ref[...], contract, preferred_element_type=jnp.float32)
        return terms[:modes] + (terms[modes : 2 * modes] + terms[2 * modes : 3 * modes])

    own, other = modal(own_ref), modal(other_ref)
    first = jnp.logical_not(is_second())
    span = own.shape[1]
    out_ref[:, :span] = jnp.where(first, own, other).astype(out_ref.dtype)
    out_ref[:, span:] = jnp.where(first, other, own).astype(out_ref.dtype)


def hankel_rows(tiles, following):
    lane = lax.broadcasted_iota(jnp.int32, (SUB, LANES), 1)
    moved = [[pltpu.roll(tile, LANES - STEP * j, 1) for j in range(1, PER_TILE)] for tile in [*tiles, following]]
    for t, tile in enumerate(tiles):
        rows = [tile] + [
            jnp.where(lane < LANES - STEP * j, moved[t][j - 1], moved[t + 1][j - 1]) for j in range(1, PER_TILE)
        ]
        yield jnp.concatenate(rows, axis=0)


def banded_product(total, hankel, first, toeplitz_ref, steps, out_tiles):
    rows = total.shape[0]
    for c in steps:
        left = jnp.concatenate(
            [hankel[c + k - first : c + k - first + out_tiles].reshape(rows, LANES) for k in range(2)], axis=1
        )
        total = total + lax.dot_general(
            left,
            toeplitz_ref[:, LANES * c : LANES * (c + 2)],
            (((1,), (1,)), ((), ())),
            preferred_element_type=jnp.float32,
        )
    return total


def near_kernel(out_tiles, back1_ref, pair_ref, taps_ref, formed_ref, total_ref, hankel_ref, toeplitz_ref):
    del formed_ref

    @pl.when(is_second())
    def _():
        fill_toeplitz(taps_ref.shape[1] // LANES, toeplitz_ref.shape[1], taps_ref, toeplitz_ref)

    chip = lax.axis_index("tm") // 2
    newer = jnp.where(chip >= 1, back1_ref[...].astype(jnp.float32), 0.0)
    every = jnp.concatenate([newer, pair_ref[...].astype(jnp.float32)], axis=1)

    def give(first):
        count = toeplitz_ref.shape[1] // LANES + out_tiles - 2 - first
        tiles = [every[:, LANES * t : LANES * (t + 1)] for t in range(count)]
        for t, rows in enumerate(hankel_rows(tiles, jnp.zeros((SUB, LANES), jnp.float32))):
            hankel_ref[first - out_tiles + t] = rows.astype(hankel_ref.dtype)
        for t in range(first - out_tiles + count, hankel_ref.shape[0]):
            hankel_ref[t] = jnp.zeros(hankel_ref.shape[1:], hankel_ref.dtype)
        steps = range(first, toeplitz_ref.shape[1] // LANES, 2)
        nothing = jnp.zeros(total_ref.shape, jnp.float32)
        total_ref[...] = banded_product(nothing, hankel_ref, out_tiles, toeplitz_ref, steps, out_tiles)

    pl.when(is_second())(lambda: give(out_tiles))
    pl.when(jnp.logical_not(is_second()))(lambda: give(2 * out_tiles))


def far_kernel(
    out_tiles, copies, back2_ref, back1_ref, near_ref, near_hankel_ref, toeplitz_ref, out_ref, hankel, total_ref
):
    chip = lax.axis_index("tm") // 2
    modes = out_ref.shape[1]
    older = jnp.where(chip >= 2, back2_ref[...].astype(jnp.float32), 0.0)
    following = jnp.where(chip >= 1, back1_ref[:, :LANES].astype(jnp.float32), 0.0)

    def add(first):
        start = 2 * out_tiles - first
        tiles = [older[:, LANES * t : LANES * (t + 1)] for t in range(start, 2 * out_tiles)]
        for t, rows in enumerate(hankel_rows(tiles, following)):
            hankel[t] = rows.astype(hankel.dtype)
        hankel[first : first + out_tiles] = near_hankel_ref[first - out_tiles : first]
        total_ref[...] = banded_product(near_ref[...], hankel, 0, toeplitz_ref, range(0, first, 2), out_tiles)

    pl.when(is_second())(lambda: add(out_tiles))
    pl.when(jnp.logical_not(is_second()))(lambda: add(2 * out_tiles))
    total = total_ref[...]
    lane = lax.broadcasted_iota(jnp.int32, (SUB, LANES), 1)
    sub = lax.broadcasted_iota(jnp.int32, (SUB, LANES), 0)
    place_in_tile, column = sub % PER_TILE, lane // STEP
    for g in range(out_tiles):
        picked = []
        for j in range(PER_TILE):
            row = (g * PER_TILE + j) * modes
            block = total[row : row + modes]
            own = block[:, :LANES]
            for h in range(1, STEP * modes // LANES):
                own = jnp.where(sub // PER_TILE == h, block[:, LANES * h : LANES * (h + 1)], own)
            picked.append(own)
        tile = jnp.zeros((SUB, LANES), jnp.float32)
        for d in range(PER_TILE):
            line = picked[d]
            for s in range(1, PER_TILE):
                line = jnp.where(place_in_tile == s, picked[(s + d) % PER_TILE], line)
            if d:
                line = pltpu.roll(line, STEP * d, 1)
            tile = jnp.where(column == (place_in_tile + d) % PER_TILE, line, tile)
        tile = tile.astype(out_ref.dtype)
        for k in range(copies):
            out_ref[k, :, LANES * g : LANES * (g + 1)] = tile


def sag_kernel(responses_ref, modes_ref, out_hbm, blocks_ref, sems):
    blocks, span = blocks_ref.shape[:2]
    modes = modes_ref[...]
    copies = []
    for k in range(blocks):
        part = responses_ref[:, :, span * k : span * (k + 1)].reshape(modes.shape[1], span)
        product = lax.dot_general(part, modes, (((0,), (1,)), ((), ())), preferred_element_type=jnp.float32)
        blocks_ref[k] = product.astype(blocks_ref.dtype)
        copies.append(pltpu.make_async_copy(blocks_ref.at[k], out_hbm.at[pl.ds(span * k, span)], sems.at[k]))
        copies[-1].start()
    for copy in copies:
        copy.wait()


def on_chip(kernel, shape, dtype, scratch=(), flops=0, bytes_accessed=0):
    return pl.pallas_call(
        kernel,
        out_shape=jax.ShapeDtypeStruct(shape, dtype),
        scratch_shapes=scratch,
        compiler_params=pltpu.CompilerParams(vmem_limit_bytes=40 * 1024 * 1024),
        cost_estimate=pl.CostEstimate(flops=flops, bytes_accessed=bytes_accessed, transcendentals=0),
    )


def per_device(ports, steps, counters, signatures, eigen_vectors_at_pins, taps):
    modes, span = taps.shape
    cycles, tallies = counters.shape
    swap = [(i, i ^ 1) for i in range(steps)]
    other = lax.ppermute(counters, "tm", swap)
    in_hbm = pl.BlockSpec(memory_space=pltpu.HBM)
    in_vmem = pl.BlockSpec(memory_space=pltpu.VMEM)
    depth = span + 2 * LANES
    partial, held, formed = pl.pallas_call(
        merging_kernel,
        out_shape=(
            jax.ShapeDtypeStruct((ports, modes, tallies), jnp.bfloat16),
            jax.ShapeDtypeStruct(counters.shape, counters.dtype),
            jax.ShapeDtypeStruct((STEP * modes, depth), jnp.bfloat16),
        ),
        in_specs=[in_hbm] * 4,
        out_specs=(in_vmem,) * 3,
        scratch_shapes=[
            pltpu.VMEM(signatures.shape, signatures.dtype),
            pltpu.VMEM(eigen_vectors_at_pins.shape, eigen_vectors_at_pins.dtype),
            pltpu.VMEM(taps.shape, taps.dtype),
            pltpu.SemaphoreType.DMA((4,)),
        ],
        compiler_params=pltpu.CompilerParams(vmem_limit_bytes=16 * 1024 * 1024),
    )(*[pltpu.with_memory_space_constraint(x, pltpu.HBM) for x in (signatures, eigen_vectors_at_pins, counters, taps)])
    parts = lax.all_to_all(partial, "port", 0, 0, tiled=True)
    tap_tiles = span // LANES
    pair = on_chip(projection_kernel, (modes, 2 * cycles), jnp.bfloat16)(parts, held, other)
    back2 = lax.ppermute(pair, "tm", [(i, (i + 4) % steps) for i in range(steps)])
    back1 = lax.ppermute(pair, "tm", [(i, (i + 2) % steps) for i in range(steps)])
    out_tiles = cycles // LANES
    rows = STEP * modes
    near, near_hankel, toeplitz = pl.pallas_call(
        functools.partial(near_kernel, out_tiles),
        out_shape=(
            jax.ShapeDtypeStruct((out_tiles * PER_TILE * modes, rows), jnp.float32),
            jax.ShapeDtypeStruct((tap_tiles + 2, PER_TILE * modes, LANES), jnp.bfloat16),
            jax.ShapeDtypeStruct((rows, depth), jnp.bfloat16),
        ),
        input_output_aliases={3: 2},
        compiler_params=pltpu.CompilerParams(vmem_limit_bytes=40 * 1024 * 1024),
        cost_estimate=pl.CostEstimate(flops=2 * 10**9, bytes_accessed=4 * rows * depth, transcendentals=0),
    )(back1, pair, taps, formed)
    responses = on_chip(
        functools.partial(far_kernel, out_tiles, ports),
        (ports, modes, cycles),
        jnp.bfloat16,
        scratch=[
            pltpu.VMEM((3 * out_tiles, PER_TILE * modes, LANES), jnp.bfloat16),
            pltpu.VMEM((out_tiles * PER_TILE * modes, rows), jnp.float32),
        ],
    )(back2, back1, near, near_hankel, toeplitz)
    complete = lax.all_to_all(responses, "port", 0, 0, tiled=True)
    local_ports = eigen_vectors_at_pins.shape[0]
    blocks = 4
    return pl.pallas_call(
        sag_kernel,
        out_shape=jax.ShapeDtypeStruct((cycles, local_ports), jnp.bfloat16),
        in_specs=[in_vmem] * 2,
        out_specs=pl.BlockSpec(memory_space=pltpu.HBM),
        scratch_shapes=[
            pltpu.VMEM((blocks, cycles // blocks, local_ports), jnp.bfloat16),
            pltpu.SemaphoreType.DMA((blocks,)),
        ],
        compiler_params=pltpu.CompilerParams(vmem_limit_bytes=16 * 1024 * 1024),
    )(complete, eigen_vectors_at_pins)


def solution(mesh):
    in_specs = (P("tm", None), P(None, "port"), P("port", None), P("port", None))
    body = functools.partial(per_device, mesh.shape["port"], mesh.shape["tm"])
    return jax.shard_map(body, mesh=mesh, in_specs=in_specs, out_specs=P("tm", "port"), check_vma=False)
```
